32 devices in a mesh: groups: 2 (over y), expert: 4 (over z), section: 4 (over x, core).
Axes of the slice: x: 2, y: 2, z: 4, core: 2. Of those that a mesh axis runs over, the one named last changes fastest.
Arguments:
- pending_microgroups: bfloat16 [4, 1024, 768], P('section', ('groups', 'expert')), parts along dimension 1, may hold values from -6 to 6
- arriving_microgroups: bfloat16 [2, 1024, 768], P(None, ('groups', 'expert')), parts along dimension 1, may hold values from -6 to 6
- expert_choice_grid: int32 [3, 4, 1024], P(None, 'section', ('groups', 'expert')), parts along dimension 2, may hold values from 0 to 1, as said below
- rootmean_gain: float32 [4, 768], P('section'), may hold values from 0.5 to 1.5
- gating_columns: bfloat16 [4, 768, 2], P('section'), may hold values from -0.21875 to 0.21875
- up_projection_matrix: bfloat16 [4, 4, 768, 768], P('section', 'expert'), may hold values from -0.21875 to 0.21875
- down_projection_matrix: bfloat16 [4, 4, 768, 768], P('section', 'expert'), may hold values from -0.21875 to 0.21875
Outputs:
- section_out: bfloat16 [4, 3, 1024, 768], P('section', None, ('groups', 'expert')), parts along dimension 2
The draws below stay inside these ranges and needn't reach their ends.
There are 2 independent parts, one for each index of `groups`. The reference program is written for one: setup_inputs(seed, part) draws one part's arguments, and reference() takes and returns one part's arrays. A program takes and returns all parts, laid end to end along the dimension named above; an argument that names none is the same for every part. Nothing has to cross between parts.
Inputs may be any that keep to these rules, and one draw needn't show every extreme that they name: `expert_choice_grid`: for every tick and section, no expert is named by more than 128 tokens of one aligned block of 128 tokens (the tokens of one device), and one expert, drawn from the seed, is named by exactly 128 tokens of every such block.
All inputs are finite; a program needn't handle non-finite values.
Results may differ from the reference program's by a relative error of at most 0.0095.
Values may be sent and summed in bfloat16 or wider, within the bound.
A program may use at most 64 MiB of HBM per device.

```python
import jax
import jax.numpy as jnp
from jax import lax

EMBED_DIMENSION = 768
TICKS = 3
ROWS_DEV = 128
HID = 768
EXPERTS = 2
LEG_TOTAL = 4
MICRO_GROUP_SIZE = 512
CAP = 128
N_EXPERT = 4


def draw_expert_choice_grid(key, part):
    key = jax.random.fold_in(key, 11)
    blocks = MICRO_GROUP_SIZE // ROWS_DEV
    remain = ROWS_DEV - CAP
    others = max(EXPERTS - 1, 1)
    per_label = -(-remain // others)
    keep_limit = CAP - per_label
    position = jnp.arange(ROWS_DEV, dtype=jnp.int32)

    def one_block(block_key, hot_expert):
        key_pick, key_perm = jax.random.split(block_key)
        picked = jax.random.randint(key_pick, (ROWS_DEV,), 0, others, dtype=jnp.int32)
        in_rest = (position >= CAP).astype(jnp.int32)
        one_hot = (picked[:, None] == jnp.arange(others, dtype=jnp.int32)[None, :]).astype(jnp.int32) * in_rest[:, None]
        label_rank = jnp.sum((jnp.cumsum(one_hot, axis=0) - one_hot) * one_hot, axis=1)
        cyclic = (position - CAP) % others
        labels = jnp.where(label_rank < keep_limit, picked, cyclic)
        other_expert = labels + (labels >= hot_expert).astype(jnp.int32)
        chosen = jnp.where(position < CAP, hot_expert, other_expert)
        return chosen[jax.random.permutation(key_perm, ROWS_DEV)]

    def one_group(group_key):
        hot_key, rest_key = jax.random.split(group_key)
        hot_expert = jax.random.randint(hot_key, (), 0, EXPERTS, dtype=jnp.int32)
        block_keys = jax.random.split(rest_key, blocks)
        return jax.vmap(one_block, in_axes=(0, None))(block_keys, hot_expert).reshape(MICRO_GROUP_SIZE)
    group_keys = jax.random.split(key, TICKS * LEG_TOTAL)
    return jax.vmap(one_group)(group_keys).reshape(TICKS, LEG_TOTAL, MICRO_GROUP_SIZE).astype(jnp.int32)


def steps_of(rng, dims, cuts, smallest, high):
    gain, own = 1.0, jax.random.fold_in(rng, 6)
    for dim, blocks in cuts:
        draws = jnp.exp(jax.random.uniform(jax.random.fold_in(own, dim), (blocks,), jnp.float32, smallest / len(cuts), high / len(cuts)))
        gain = gain * jnp.repeat(draws, dims[dim] // blocks).reshape([-1 if axis == dim else 1 for axis in range(len(dims))])
    return gain


def normal_values(stream_key, dims, width, bound, cuts=(), kind=jnp.bfloat16):
    loudness = steps_of(stream_key, dims, cuts, -0.22, 0.18) if cuts else 1.0
    values = jax.random.normal(stream_key, dims, jnp.float32) * width * loudness
    return jnp.minimum(jnp.maximum(values, -bound), bound).astype(kind)


def setup_inputs(seed: int = 0, part: int = 0) -> dict:
    seeds = jax.random.split(jax.random.key(seed), 8)
    own_keys = jax.random.split(jax.random.fold_in(seeds[7], part), 8)
    pending_microgroups = normal_values(own_keys[0], (LEG_TOTAL, MICRO_GROUP_SIZE, EMBED_DIMENSION), 1.0, 6.0, ((0, 4), (1, 4)))
    arriving_microgroups = normal_values(own_keys[1], (TICKS - 1, MICRO_GROUP_SIZE, EMBED_DIMENSION), 1.0, 6.0, ((1, 4),))
    expert_choice_grid = draw_expert_choice_grid(jax.random.fold_in(jax.random.fold_in(seeds[7], part), 71), part)
    rootmean_gain = jnp.clip(1.0 + 0.1 * jax.random.normal(seeds[3], (LEG_TOTAL, EMBED_DIMENSION), jnp.float32), 0.5, 1.5)
    gating_columns = normal_values(seeds[4], (LEG_TOTAL, EMBED_DIMENSION, EXPERTS), EMBED_DIMENSION ** -0.5, 0.21875, ((0, 4),))
    up_projection_matrix = normal_values(seeds[5], (LEG_TOTAL, 2 * EXPERTS, EMBED_DIMENSION, HID), EMBED_DIMENSION ** -0.5, 0.21875, ((0, 4), (1, 4)))
    down_projection_matrix = normal_values(seeds[6], (LEG_TOTAL, 2 * EXPERTS, HID, EMBED_DIMENSION), HID ** -0.5, 0.21875, ((0, 4), (1, 4)))
    return dict(pending_microgroups=pending_microgroups, arriving_microgroups=arriving_microgroups, expert_choice_grid=expert_choice_grid, rootmean_gain=rootmean_gain, gating_columns=gating_columns, up_projection_matrix=up_projection_matrix, down_projection_matrix=down_projection_matrix)


def expert_layer(tok_rows, routes, rootmean_gain, gating_columns, up_projection_matrix, down_projection_matrix):
    float_rows = tok_rows.astype(jnp.float32)
    inv_rms = lax.rsqrt(lax.optimization_barrier(jnp.mean(float_rows * float_rows, axis=-1, keepdims=True)) + 1e-06)
    normed = (float_rows * inv_rms * rootmean_gain.astype(jnp.float32)).astype(jnp.bfloat16)
    logits = jnp.dot(normed, gating_columns, preferred_element_type=jnp.float32)
    gate_value = jax.nn.sigmoid(jnp.take_along_axis(logits, routes[:, None].astype(jnp.int32), axis=1)[:, 0])
    row_limit = N_EXPERT * CAP

    def per_expert(expert):
        chosen = routes == expert
        row_index = jnp.nonzero(chosen, size=row_limit, fill_value=0)[0].astype(jnp.int32)
        is_valid = jnp.arange(row_limit, dtype=jnp.int32) < jnp.sum(chosen.astype(jnp.int32))
        picked = normed[row_index]
        partials = []
        for half_idx in range(2):
            hidden = jnp.maximum(jnp.dot(picked, up_projection_matrix[2 * expert + half_idx], preferred_element_type=jnp.float32), 0.0).astype(jnp.bfloat16)
            partials.append(jnp.dot(hidden, down_projection_matrix[2 * expert + half_idx], preferred_element_type=jnp.float32).astype(jnp.bfloat16))
        merged = (partials[0].astype(jnp.float32) + partials[1].astype(jnp.float32)).astype(jnp.bfloat16)
        merged = lax.optimization_barrier(merged)
        return (row_index, jnp.where(is_valid[:, None], merged.astype(jnp.float32), jnp.float32(0.0)))
    row_index, values = lax.map(per_expert, jnp.arange(EXPERTS, dtype=jnp.int32))
    expert_out = jnp.zeros(float_rows.shape, jnp.float32).at[row_index.reshape(-1)].add(values.reshape(-1, EMBED_DIMENSION))
    return (float_rows + gate_value[:, None] * expert_out).astype(jnp.bfloat16)

def reference(pending_microgroups, arriving_microgroups, expert_choice_grid, rootmean_gain, gating_columns, up_projection_matrix, down_projection_matrix):
    running_activation = [pending_microgroups[leg_position] for leg_position in range(LEG_TOTAL)]
    per_tick = []
    for tick_idx in range(TICKS):
        outputs = [expert_layer(running_activation[leg_position], expert_choice_grid[tick_idx, leg_position], rootmean_gain[leg_position], gating_columns[leg_position], up_projection_matrix[leg_position], down_projection_matrix[leg_position]) for leg_position in range(LEG_TOTAL)]
        per_tick.append(jnp.stack(outputs))
        if tick_idx + 1 < TICKS:
            running_activation = [arriving_microgroups[tick_idx]] + outputs[:-1]
    return jnp.stack(per_tick, axis=1)
```

```python
import functools

import jax
import jax.numpy as jnp
from jax import lax
from jax.experimental import pallas as pl
from jax.experimental.pallas import tpu as pltpu
from jax.sharding import PartitionSpec as P

TICKS = 3


def swapped(x, axis, bit):
    return lax.ppermute(x, axis, [(i, i ^ 1 << bit) for i in range(lax.axis_size(axis))])


def from_behind(value, axis, steps):
    count = lax.axis_size(axis)
    initial, last = (max(0, -steps), min(count, count - steps))
    return lax.ppermute(value, axis, [(source, source + steps) for source in range(initial, last)])


def half_output(received, up_projection_matrix, down_projection_matrix):
    hidden = jnp.maximum(
        jnp.einsum(
            "sid,dh->sih", received, up_projection_matrix, preferred_element_type=jnp.float32
        ),
        0.0,
    ).astype(jnp.bfloat16)
    return jnp.einsum(
        "sih,hd->sid", hidden, down_projection_matrix, preferred_element_type=jnp.float32
    ).astype(jnp.bfloat16)


def expert_layer(
    tok_rows,
    routes,
    rootmean_gain,
    gating_columns,
    up_projection_matrix,
    down_projection_matrix,
    other_in,
    other_out,
):
    num_rows, width = tok_rows.shape
    experts = gating_columns.shape[1]
    capacity = min(num_rows, 3 * num_rows // experts)
    float_rows = tok_rows.astype(jnp.float32)
    inv_rms = lax.rsqrt(jnp.mean(float_rows * float_rows, axis=-1, keepdims=True) + 1e-06)
    normed = (float_rows * inv_rms * rootmean_gain).astype(jnp.bfloat16)
    logits = jnp.dot(normed, gating_columns, preferred_element_type=jnp.float32)
    one_hot = routes[:, None] == jnp.arange(experts, dtype=jnp.int32)[None, :]
    gate_value = jax.nn.sigmoid(jnp.sum(jnp.where(one_hot, logits, 0.0), axis=1))
    order = jnp.arange(num_rows, dtype=jnp.int32)
    same_before = (routes[:, None] == routes[None, :]) & (order[:, None] > order[None, :])
    slot_rank = jnp.sum(same_before.astype(jnp.int32), axis=1)
    slot_index = routes * capacity + slot_rank
    placing = (
        slot_index[None, :] == jnp.arange(experts * capacity, dtype=jnp.int32)[:, None]
    ).astype(jnp.bfloat16)
    outgoing = jnp.dot(placing, normed, preferred_element_type=jnp.float32).astype(jnp.bfloat16)
    outgoing = outgoing.reshape(experts, capacity, width)
    halves = outgoing.reshape(2 * experts, capacity // 2, width)
    received = lax.all_to_all(halves, "expert", split_axis=0, concat_axis=0, tiled=True)
    own_part = half_output(received, up_projection_matrix, down_projection_matrix)
    other_part = half_output(received, other_in, other_out)
    summed = (own_part.astype(jnp.float32) + other_part.astype(jnp.float32)).astype(jnp.bfloat16)
    combined = lax.all_to_all(summed, "expert", split_axis=0, concat_axis=0, tiled=True)
    flat_out = combined.reshape(experts * capacity, width)
    expert_out = lax.dot_general(
        placing, flat_out, (((0,), (0,)), ((), ())), preferred_element_type=jnp.float32
    )
    return (float_rows + gate_value[:, None] * expert_out).astype(jnp.bfloat16)


def per_device(
    pending_microgroups,
    arriving_microgroups,
    expert_choice_grid,
    rootmean_gain,
    gating_columns,
    up_projection_matrix,
    down_projection_matrix,
):
    leg_position = lax.axis_index("section")
    own_in = up_projection_matrix[0, 0]
    own_out = down_projection_matrix[0, 0]
    other_in, other_out = swapped((own_in, own_out), "expert", 0)
    running_activation = pending_microgroups[0]
    per_tick = []
    for tick_idx in range(TICKS):
        layer_out = expert_layer(
            running_activation,
            expert_choice_grid[tick_idx, 0],
            rootmean_gain[0],
            gating_columns[0],
            own_in,
            own_out,
            other_in,
            other_out,
        )
        per_tick.append(layer_out)
        if tick_idx + 1 < TICKS:
            moved = from_behind(layer_out, "section", 1)
            running_activation = jnp.where(leg_position == 0, arriving_microgroups[tick_idx], moved)
    return jnp.stack(per_tick)[None]


MESH = pl.DeviceIdType.MESH
IN_FLIGHT = 3


def column_of(row):
    count = row.shape[1]
    down = lax.broadcasted_iota(jnp.int32, (count, count), 0)
    along = lax.broadcasted_iota(jnp.int32, (count, count), 1)
    return jnp.sum(jnp.where(down == along, row, 0.0), axis=1, keepdims=True)


def relay_kernel(
    sections,
    cut,
    pending,
    arriving,
    routes,
    gain,
    gating,
    up,
    down,
    out,
    x,
    part,
    their_part,
    y_out,
    ids,
    own_up,
    own_down,
    far_up,
    far_down,
    own_sum,
    hidden,
    gate,
    load_sem,
    x_sem,
    up_sem,
    up_share_sem,
    down_sem,
    down_share_sem,
    part_sem,
    relay_sem,
):
    ticks = out.shape[1]
    rows, width = out.shape[2:]
    hid = up.shape[3]
    up_cut = up_sem.shape[1]
    group = lax.axis_index("groups")
    place = lax.axis_index("expert")
    section = lax.axis_index("section")
    slot = lax.rem(place, 2)
    own_expert = place // 2
    mate = {"expert": place + 1 - 2 * slot}
    across = {"expert": lax.rem(place + 2, 4)}
    twin = {"groups": 1 - group}
    ahead = {"section": jnp.minimum(section + 1, sections - 1)}
    behind = {"section": jnp.maximum(section - 1, 0)}
    first = section == 0
    has_ahead = section < sections - 1
    has_behind = section > 0

    def remote(source, target, sems, index, device):
        return pltpu.make_async_remote_copy(
            src_ref=source,
            dst_ref=target,
            send_sem=sems.at[(0, *index)],
            recv_sem=sems.at[(1, *index)],
            device_id=device,
            device_id_type=MESH,
        )

    half = width // 2
    my_half = pl.multiple_of(group * half, half)
    twin_half = pl.multiple_of((1 - group) * half, half)
    hid_half = hid // 2
    my_hid = pl.multiple_of(group * hid_half, hid_half)
    twin_hid = pl.multiple_of((1 - group) * hid_half, hid_half)
    wide = width // cut
    piece = half // up_cut

    def up_rows(begin, k):
        return pl.ds(pl.multiple_of(begin + k * piece, piece), piece)

    loads = [
        pltpu.make_async_copy(up.at[0, 0], own_up, load_sem.at[0]),
        pltpu.make_async_copy(down.at[0, 0], own_down, load_sem.at[1]),
        pltpu.make_async_copy(pending.at[0], x.at[0, slot], load_sem.at[2]),
    ]
    arrivals = [
        pltpu.make_async_copy(arriving.at[t], x.at[t + 1, slot], load_sem.at[3 + t])
        for t in range(ticks - 1)
    ]
    for load in loads:
        load.start()

    @pl.when(first)
    def _():
        for load in arrivals:
            load.start()

    barrier = pltpu.get_barrier_semaphore()
    for device in (mate, across, twin):
        pl.semaphore_signal(barrier, inc=1, device_id=device, device_id_type=MESH)

    @pl.when(has_ahead)
    def _():
        pl.semaphore_signal(barrier, inc=1, device_id=ahead, device_id_type=MESH)

    @pl.when(has_behind)
    def _():
        pl.semaphore_signal(barrier, inc=1, device_id=behind, device_id_type=MESH)

    pl.semaphore_wait(barrier, 3 + has_ahead.astype(jnp.int32) + has_behind.astype(jnp.int32))

    route_copy = remote(routes, ids, x_sem, (0,), mate)
    token_copy = remote(pending.at[0], x.at[0, slot], x_sem, (1,), mate)
    arrival_copies = [
        remote(arriving.at[t], x.at[t + 1, slot], x_sem, (2 + t,), mate) for t in range(ticks - 1)
    ]
    route_copy.start()
    token_copy.start()

    sends, shares = [], []
    for k in range(up_cut):
        mine = up_rows(my_half, k)
        sends.append(remote(up.at[0, 0, mine], far_up.at[mine], up_sem, (k,), across))
        shares.append(remote(far_up.at[mine], far_up.at[mine], up_share_sem, (k,), twin))
    for c in range(cut):
        mine = (pl.ds(my_hid, hid_half), pl.ds(c * wide, wide))
        sends.append(remote(down.at[(0, 0, *mine)], far_down.at[mine], down_sem, (c,), across))
        shares.append(remote(far_down.at[mine], far_down.at[mine], down_share_sem, (c,), twin))
    for send in sends[:IN_FLIGHT]:
        send.start()

    def take(k):
        sends[k].wait_recv()
        shares[k].start()
        if k + IN_FLIGHT < len(sends):
            sends[k].wait_send()
            sends[k + IN_FLIGHT].start()

    loads[2].wait()
    route_copy.wait()
    token_copy.wait()

    @pl.when(first)
    def _():
        for copy in arrival_copies:
            copy.start()

    both = (2 * rows, width)
    gains = gain[...]
    columns = gating[0]

    def owners(t):
        mine, theirs = (
            column_of(ref[t].astype(jnp.float32)) for ref in (routes, ids)
        )
        return jnp.concatenate(
            [jnp.where(slot == 0, mine, theirs), jnp.where(slot == 0, theirs, mine)], axis=0
        )

    def prepare(t):
        rows_f32 = x[t].reshape(both).astype(jnp.float32)
        inv_rms = lax.rsqrt(jnp.mean(rows_f32 * rows_f32, axis=-1, keepdims=True) + 1e-06)
        normed = (rows_f32 * inv_rms * gains).astype(jnp.bfloat16)
        owner = owners(t)
        logits = jnp.dot(normed, columns, preferred_element_type=jnp.float32)
        names = lax.broadcasted_iota(jnp.int32, logits.shape, 1).astype(jnp.float32)
        logit = jnp.sum(jnp.where(owner == names, logits, 0.0), axis=1, keepdims=True)
        gate[...] = jax.nn.sigmoid(logit)
        return normed, owner == own_expert.astype(jnp.float32)

    def hidden_of(normed, weights, kept):
        value = jnp.dot(normed, weights, preferred_element_type=jnp.float32)
        return jnp.where(kept, jnp.maximum(value, 0.0), 0.0).astype(jnp.bfloat16)

    def part_copy(t, c):
        span = pl.ds(c * wide, wide)
        if t + 1 < ticks:
            here = (t, slice(None), slice(None), span)
        else:
            here = (t, 1 - slot, slice(None), span)
        return remote(part.at[here], their_part.at[here], part_sem, (t, c), mate)

    def relay_copy(t, c):
        span = (slice(None), slice(None), pl.ds(c * wide, wide))
        return remote(y_out.at[(t, *span)], x.at[(t + 1, *span)], relay_sem, (t, c), ahead)

    def put_part(t, c, value):
        part[t, :, :, c * wide : (c + 1) * wide] = value.astype(jnp.bfloat16).reshape(2, rows, wide)
        part_copy(t, c).start()

    def finish(t, c):
        part_copy(t, c).wait_recv()
        span = slice(c * wide, (c + 1) * wide)
        if t + 1 < ticks:
            summed = part[t, :, :, span].astype(jnp.float32) + their_part[
                t, :, :, span
            ].astype(jnp.float32)
            summed = summed.astype(jnp.bfloat16).astype(jnp.float32)
            gates = gate[...].reshape(2, rows, 1)
            y_out[t, :, :, span] = (
                x[t, :, :, span].astype(jnp.float32) + gates * summed
            ).astype(jnp.bfloat16)

            @pl.when(has_ahead)
            def _():
                relay_copy(t, c).start()

            out[0, t, :, span] = y_out[t, slot, :, span]
        else:
            summed = part[t, slot, :, span].astype(jnp.float32) + their_part[
                t, slot, :, span
            ].astype(jnp.float32)
            summed = summed.astype(jnp.bfloat16).astype(jnp.float32)
            gates = gate[pl.ds(pl.multiple_of(slot * rows, rows), rows), :]
            out[0, t, :, span] = (
                x[t, slot, :, span].astype(jnp.float32) + gates * summed
            ).astype(jnp.bfloat16)

    normed, kept = prepare(0)
    loads[0].wait()
    hidden[:, :hid] = hidden_of(normed, own_up[...], kept)
    loads[1].wait()
    own_sum[...] = jnp.dot(hidden[:, :hid], own_down[...], preferred_element_type=jnp.float32)
    for k in range(up_cut):
        take(k)
    for k in range(up_cut):
        shares[k].wait_recv()
    hidden[:, hid:] = hidden_of(normed, far_up[...], jnp.logical_not(kept))
    take(up_cut)
    for c in range(cut):
        if c + 1 < cut:
            take(up_cut + c + 1)
        shares[up_cut + c].wait_recv()
        span = slice(c * wide, (c + 1) * wide)
        put_part(
            0,
            c,
            own_sum[:, span]
            + jnp.dot(hidden[:, hid:], far_down[:, span], preferred_element_type=jnp.float32),
        )
        if c > 0:
            finish(0, c - 1)
    finish(0, cut - 1)

    for t in range(1, ticks):

        @pl.when(first)
        def _():
            arrivals[t - 1].wait()
            arrival_copies[t - 1].wait()

        @pl.when(has_behind)
        def _():
            for c in range(cut):
                relay_copy(t - 1, c).wait_recv()

        normed, kept = prepare(t)
        hidden[:, :hid] = hidden_of(normed, own_up[...], kept)
        hidden[:, hid:] = hidden_of(normed, far_up[...], jnp.logical_not(kept))
        for c in range(cut):
            span = slice(c * wide, (c + 1) * wide)
            put_part(
                t,
                c,
                jnp.dot(hidden[:, :hid], own_down[:, span], preferred_element_type=jnp.float32)
                + jnp.dot(hidden[:, hid:], far_down[:, span], preferred_element_type=jnp.float32),
            )
        for c in range(cut):
            finish(t, c)

    for k, send in enumerate(sends):
        if k + IN_FLIGHT >= len(sends):
            send.wait_send()
    for share in shares:
        share.wait_send()
    for t in range(ticks):
        for c in range(cut):
            part_copy(t, c).wait_send()

    @pl.when(has_ahead)
    def _():
        for t in range(ticks - 1):
            for c in range(cut):
                relay_copy(t, c).wait_send()


def relay(
    sections,
    pending_microgroups,
    arriving_microgroups,
    expert_choice_grid,
    rootmean_gain,
    gating_columns,
    up_projection_matrix,
    down_projection_matrix,
):
    _, rows, width = pending_microgroups.shape
    ticks = expert_choice_grid.shape[0]
    hid = up_projection_matrix.shape[3]
    cut, up_cut = width // 128, 3
    vmem, anywhere = pl.BlockSpec(memory_space=pltpu.VMEM), pl.BlockSpec(memory_space=pl.ANY)
    sems = pltpu.SemaphoreType.DMA
    return pl.pallas_call(
        functools.partial(relay_kernel, sections, cut),
        out_shape=jax.ShapeDtypeStruct((1, ticks, rows, width), jnp.bfloat16),
        in_specs=[anywhere, anywhere, vmem, vmem, vmem, anywhere, anywhere],
        out_specs=vmem,
        scratch_shapes=[
            pltpu.VMEM((ticks, 2, rows, width), jnp.bfloat16),
            pltpu.VMEM((ticks, 2, rows, width), jnp.bfloat16),
            pltpu.VMEM((ticks, 2, rows, width), jnp.bfloat16),
            pltpu.VMEM((ticks - 1, 2, rows, width), jnp.bfloat16),
            pltpu.VMEM((ticks, 1, rows), jnp.int32),
            pltpu.VMEM((width, hid), jnp.bfloat16),
            pltpu.VMEM((hid, width), jnp.bfloat16),
            pltpu.VMEM((width, hid), jnp.bfloat16),
            pltpu.VMEM((hid, width), jnp.bfloat16),
            pltpu.VMEM((2 * rows, width), jnp.float32),
            pltpu.VMEM((2 * rows, 2 * hid), jnp.bfloat16),
            pltpu.VMEM((2 * rows, 1), jnp.float32),
            sems((2 + ticks,)),
            sems((2, 1 + ticks)),
            sems((2, up_cut)),
            sems((2, up_cut)),
            sems((2, cut)),
            sems((2, cut)),
            sems((2, ticks, cut)),
            sems((2, ticks - 1, cut)),
        ],
        compiler_params=pltpu.CompilerParams(
            collective_id=0, has_side_effects=True, vmem_limit_bytes=48 * 2**20
        ),
    )(
        pending_microgroups,
        arriving_microgroups,
        expert_choice_grid,
        rootmean_gain,
        gating_columns,
        up_projection_matrix,
        down_projection_matrix,
    )


def solution(mesh):
    placed = (
        P("section", ("groups", "expert"), None),
        P(None, ("groups", "expert"), None),
        P(None, "section", ("groups", "expert")),
        P("section", None),
        P("section", None, None),
        P("section", "expert", None, None),
        P("section", "expert", None, None),
    )
    shape = dict(mesh.shape)
    if shape["expert"] == 4 and shape["groups"] == 2:
        form = functools.partial(relay, shape["section"])
    else:
        form = per_device
    return jax.shard_map(
        form,
        mesh=mesh,
        in_specs=placed,
        out_specs=P("section", None, ("groups", "expert"), None),
        check_vma=False,
    )
```

```python
import functools

import jax
import jax.numpy as jnp
from jax import lax
from jax.experimental import pallas as pl
from jax.experimental.pallas import tpu as pltpu
from jax.sharding import PartitionSpec as P

TICKS = 3


def swapped(x, axis, bit):
    return lax.ppermute(x, axis, [(i, i ^ 1 << bit) for i in range(lax.axis_size(axis))])


def from_behind(value, axis, steps):
    count = lax.axis_size(axis)
    initial, last = (max(0, -steps), min(count, count - steps))
    return lax.ppermute(value, axis, [(source, source + steps) for source in range(initial, last)])


def half_output(received, up_projection_matrix, down_projection_matrix):
    hidden = jnp.maximum(
        jnp.einsum(
            "sid,dh->sih", received, up_projection_matrix, preferred_element_type=jnp.float32
        ),
        0.0,
    ).astype(jnp.bfloat16)
    return jnp.einsum(
        "sih,hd->sid", hidden, down_projection_matrix, preferred_element_type=jnp.float32
    ).astype(jnp.bfloat16)


def expert_layer(
    tok_rows,
    routes,
    rootmean_gain,
    gating_columns,
    up_projection_matrix,
    down_projection_matrix,
    other_in,
    other_out,
):
    num_rows, width = tok_rows.shape
    experts = gating_columns.shape[1]
    capacity = min(num_rows, 3 * num_rows // experts)
    float_rows = tok_rows.astype(jnp.float32)
    inv_rms = lax.rsqrt(jnp.mean(float_rows * float_rows, axis=-1, keepdims=True) + 1e-06)
    normed = (float_rows * inv_rms * rootmean_gain).astype(jnp.bfloat16)
    logits = jnp.dot(normed, gating_columns, preferred_element_type=jnp.float32)
    one_hot = routes[:, None] == jnp.arange(experts, dtype=jnp.int32)[None, :]
    gate_value = jax.nn.sigmoid(jnp.sum(jnp.where(one_hot, logits, 0.0), axis=1))
    order = jnp.arange(num_rows, dtype=jnp.int32)
    same_before = (routes[:, None] == routes[None, :]) & (order[:, None] > order[None, :])
    slot_rank = jnp.sum(same_before.astype(jnp.int32), axis=1)
    slot_index = routes * capacity + slot_rank
    placing = (
        slot_index[None, :] == jnp.arange(experts * capacity, dtype=jnp.int32)[:, None]
    ).astype(jnp.bfloat16)
    outgoing = jnp.dot(placing, normed, preferred_element_type=jnp.float32).astype(jnp.bfloat16)
    outgoing = outgoing.reshape(experts, capacity, width)
    halves = outgoing.reshape(2 * experts, capacity // 2, width)
    received = lax.all_to_all(halves, "expert", split_axis=0, concat_axis=0, tiled=True)
    own_part = half_output(received, up_projection_matrix, down_projection_matrix)
    other_part = half_output(received, other_in, other_out)
    summed = (own_part.astype(jnp.float32) + other_part.astype(jnp.float32)).astype(jnp.bfloat16)
    combined = lax.all_to_all(summed, "expert", split_axis=0, concat_axis=0, tiled=True)
    flat_out = combined.reshape(experts * capacity, width)
    expert_out = lax.dot_general(
        placing, flat_out, (((0,), (0,)), ((), ())), preferred_element_type=jnp.float32
    )
    return (float_rows + gate_value[:, None] * expert_out).astype(jnp.bfloat16)


def per_device(
    pending_microgroups,
    arriving_microgroups,
    expert_choice_grid,
    rootmean_gain,
    gating_columns,
    up_projection_matrix,
    down_projection_matrix,
):
    leg_position = lax.axis_index("section")
    own_in = up_projection_matrix[0, 0]
    own_out = down_projection_matrix[0, 0]
    other_in, other_out = swapped((own_in, own_out), "expert", 0)
    running_activation = pending_microgroups[0]
    per_tick = []
    for tick_idx in range(TICKS):
        layer_out = expert_layer(
            running_activation,
            expert_choice_grid[tick_idx, 0],
            rootmean_gain[0],
            gating_columns[0],
            own_in,
            own_out,
            other_in,
            other_out,
        )
        per_tick.append(layer_out)
        if tick_idx + 1 < TICKS:
            moved = from_behind(layer_out, "section", 1)
            running_activation = jnp.where(leg_position == 0, arriving_microgroups[tick_idx], moved)
    return jnp.stack(per_tick)[None]


MESH = pl.DeviceIdType.MESH
IN_FLIGHT = 2


def column_of(row):
    count = row.shape[1]
    down = lax.broadcasted_iota(jnp.int32, (count, count), 0)
    along = lax.broadcasted_iota(jnp.int32, (count, count), 1)
    return jnp.sum(jnp.where(down == along, row, 0.0), axis=1, keepdims=True)


def relay_kernel(
    sections,
    cut,
    pending,
    arriving,
    routes,
    gain,
    gating,
    up,
    down,
    out,
    x,
    part,
    their_part,
    y_out,
    ids,
    own_up,
    own_down,
    far_up,
    far_down,
    own_sum,
    hidden,
    gate,
    load_sem,
    x_sem,
    up_sem,
    up_share_sem,
    down_sem,
    down_share_sem,
    part_sem,
    relay_sem,
):
    ticks = out.shape[1]
    rows, width = out.shape[2:]
    hid = up.shape[3]
    up_cut = up_sem.shape[1]
    group = lax.axis_index("groups")
    place = lax.axis_index("expert")
    section = lax.axis_index("section")
    slot = lax.rem(place, 2)
    own_expert = place // 2
    mate = {"expert": place + 1 - 2 * slot}
    across = {"expert": lax.rem(place + 2, 4)}
    twin = {"groups": 1 - group}
    ahead = {"section": jnp.minimum(section + 1, sections - 1)}
    behind = {"section": jnp.maximum(section - 1, 0)}
    first = section == 0
    has_ahead = section < sections - 1
    has_behind = section > 0

    def remote(source, target, sems, index, device):
        return pltpu.make_async_remote_copy(
            src_ref=source,
            dst_ref=target,
            send_sem=sems.at[(0, *index)],
            recv_sem=sems.at[(1, *index)],
            device_id=device,
            device_id_type=MESH,
        )

    half = width // 2
    my_half = pl.multiple_of(group * half, half)
    twin_half = pl.multiple_of((1 - group) * half, half)
    hid_half = hid // 2
    my_hid = pl.multiple_of(group * hid_half, hid_half)
    twin_hid = pl.multiple_of((1 - group) * hid_half, hid_half)
    wide = width // cut
    piece = half // up_cut

    def up_rows(begin, k):
        return pl.ds(pl.multiple_of(begin + k * piece, piece), piece)

    loads = [
        pltpu.make_async_copy(up.at[0, 0], own_up, load_sem.at[0]),
        pltpu.make_async_copy(down.at[0, 0], own_down, load_sem.at[1]),
        pltpu.make_async_copy(pending.at[0], x.at[0, slot], load_sem.at[2]),
    ]
    arrivals = [
        pltpu.make_async_copy(arriving.at[t], x.at[t + 1, slot], load_sem.at[3 + t])
        for t in range(ticks - 1)
    ]
    for load in loads:
        load.start()

    @pl.when(first)
    def _():
        for load in arrivals:
            load.start()

    barrier = pltpu.get_barrier_semaphore()
    for device in (mate, across, twin):
        pl.semaphore_signal(barrier, inc=1, device_id=device, device_id_type=MESH)

    @pl.when(has_ahead)
    def _():
        pl.semaphore_signal(barrier, inc=1, device_id=ahead, device_id_type=MESH)

    @pl.when(has_behind)
    def _():
        pl.semaphore_signal(barrier, inc=1, device_id=behind, device_id_type=MESH)

    pl.semaphore_wait(barrier, 3 + has_ahead.astype(jnp.int32) + has_behind.astype(jnp.int32))

    route_copy = remote(routes, ids, x_sem, (0,), mate)
    token_copy = remote(pending.at[0], x.at[0, slot], x_sem, (1,), mate)
    arrival_copies = [
        remote(arriving.at[t], x.at[t + 1, slot], x_sem, (2 + t,), mate) for t in range(ticks - 1)
    ]
    route_copy.start()
    token_copy.start()

    sends, shares = [], []
    for k in range(up_cut):
        mine = up_rows(my_half, k)
        sends.append(remote(up.at[0, 0, mine], far_up.at[mine], up_sem, (k,), across))
        shares.append(remote(far_up.at[mine], far_up.at[mine], up_share_sem, (k,), twin))
    for c in range(cut):
        mine = (pl.ds(my_hid, hid_half), pl.ds(c * wide, wide))
        sends.append(remote(down.at[(0, 0, *mine)], far_down.at[mine], down_sem, (c,), across))
        shares.append(remote(far_down.at[mine], far_down.at[mine], down_share_sem, (c,), twin))
    for send in sends[:IN_FLIGHT]:
        send.start()

    def take(k):
        sends[k].wait_recv()
        shares[k].start()
        if k + IN_FLIGHT < len(sends):
            sends[k].wait_send()
            sends[k + IN_FLIGHT].start()

    loads[2].wait()
    route_copy.wait()
    token_copy.wait()

    @pl.when(first)
    def _():
        for copy in arrival_copies:
            copy.start()

    both = (2 * rows, width)
    gains = gain[...]
    columns = gating[0]

    def owners(t):
        mine, theirs = (
            column_of(ref[t].astype(jnp.float32)) for ref in (routes, ids)
        )
        return jnp.concatenate(
            [jnp.where(slot == 0, mine, theirs), jnp.where(slot == 0, theirs, mine)], axis=0
        )

    def prepare(t):
        rows_f32 = x[t].reshape(both).astype(jnp.float32)
        inv_rms = lax.rsqrt(jnp.mean(rows_f32 * rows_f32, axis=-1, keepdims=True) + 1e-06)
        normed = (rows_f32 * inv_rms * gains).astype(jnp.bfloat16)
        owner = owners(t)
        logits = lax.dot_general(
            normed, columns, (((1,), (1,)), ((), ())), preferred_element_type=jnp.float32
        )
        names = lax.broadcasted_iota(jnp.int32, logits.shape, 1).astype(jnp.float32)
        logit = jnp.sum(jnp.where(owner == names, logits, 0.0), axis=1, keepdims=True)
        gate[...] = jax.nn.sigmoid(logit)
        return normed, owner == own_expert.astype(jnp.float32)

    def hidden_of(normed, weights, kept):
        value = jnp.dot(normed, weights, preferred_element_type=jnp.float32)
        return jnp.where(kept, jnp.maximum(value, 0.0), 0.0).astype(jnp.bfloat16)

    def part_copy(t, c):
        span = pl.ds(c * wide, wide)
        if t + 1 < ticks:
            here = (t, slice(None), slice(None), span)
        else:
            here = (t, 1 - slot, slice(None), span)
        return remote(part.at[here], their_part.at[here], part_sem, (t, c), mate)

    def relay_copy(t, c):
        span = (slice(None), slice(None), pl.ds(c * wide, wide))
        return remote(y_out.at[(t, *span)], x.at[(t + 1, *span)], relay_sem, (t, c), ahead)

    def put_part(t, c, value):
        part[t, :, :, c * wide : (c + 1) * wide] = value.astype(jnp.bfloat16).reshape(2, rows, wide)
        part_copy(t, c).start()

    def finish(t, c):
        part_copy(t, c).wait_recv()
        span = slice(c * wide, (c + 1) * wide)
        if t + 1 < ticks:
            summed = part[t, :, :, span].astype(jnp.float32) + their_part[
                t, :, :, span
            ].astype(jnp.float32)
            summed = summed.astype(jnp.bfloat16).astype(jnp.float32)
            gates = gate[...].reshape(2, rows, 1)
            y_out[t, :, :, span] = (
                x[t, :, :, span].astype(jnp.float32) + gates * summed
            ).astype(jnp.bfloat16)

            @pl.when(has_ahead)
            def _():
                relay_copy(t, c).start()

            out[0, t, :, span] = y_out[t, slot, :, span]
        else:
            summed = part[t, slot, :, span].astype(jnp.float32) + their_part[
                t, slot, :, span
            ].astype(jnp.float32)
            summed = summed.astype(jnp.bfloat16).astype(jnp.float32)
            gates = gate[pl.ds(pl.multiple_of(slot * rows, rows), rows), :]
            out[0, t, :, span] = (
                x[t, slot, :, span].astype(jnp.float32) + gates * summed
            ).astype(jnp.bfloat16)

    normed, kept = prepare(0)
    loads[0].wait()
    hidden[:, :hid] = hidden_of(normed, own_up[...], kept)
    loads[1].wait()
    own_sum[...] = jnp.dot(hidden[:, :hid], own_down[...], preferred_element_type=jnp.float32)
    for k in range(up_cut):
        take(k)
    for k in range(up_cut):
        shares[k].wait_recv()
    hidden[:, hid:] = hidden_of(normed, far_up[...], jnp.logical_not(kept))
    take(up_cut)
    for c in range(cut):
        if c + 1 < cut:
            take(up_cut + c + 1)
        shares[up_cut + c].wait_recv()
        span = slice(c * wide, (c + 1) * wide)
        put_part(
            0,
            c,
            own_sum[:, span]
            + jnp.dot(hidden[:, hid:], far_down[:, span], preferred_element_type=jnp.float32),
        )
        if c > 0:
            finish(0, c - 1)
    finish(0, cut - 1)

    for t in range(1, ticks):

        @pl.when(first)
        def _():
            arrivals[t - 1].wait()
            arrival_copies[t - 1].wait()

        @pl.when(has_behind)
        def _():
            for c in range(cut):
                relay_copy(t - 1, c).wait_recv()

        normed, kept = prepare(t)
        hidden[:, :hid] = hidden_of(normed, own_up[...], kept)
        hidden[:, hid:] = hidden_of(normed, far_up[...], jnp.logical_not(kept))
        for c in range(cut):
            span = slice(c * wide, (c + 1) * wide)
            put_part(
                t,
                c,
                jnp.dot(hidden[:, :hid], own_down[:, span], preferred_element_type=jnp.float32)
                + jnp.dot(hidden[:, hid:], far_down[:, span], preferred_element_type=jnp.float32),
            )
        for c in range(cut):
            finish(t, c)

    for k, send in enumerate(sends):
        if k + IN_FLIGHT >= len(sends):
            send.wait_send()
    for share in shares:
        share.wait_send()
    for t in range(ticks):
        for c in range(cut):
            part_copy(t, c).wait_send()

    @pl.when(has_ahead)
    def _():
        for t in range(ticks - 1):
            for c in range(cut):
                relay_copy(t, c).wait_send()


def relay(
    sections,
    pending_microgroups,
    arriving_microgroups,
    expert_choice_grid,
    rootmean_gain,
    gating_columns,
    up_projection_matrix,
    down_projection_matrix,
):
    _, rows, width = pending_microgroups.shape
    ticks = expert_choice_grid.shape[0]
    hid = up_projection_matrix.shape[3]
    cut, up_cut = width // 128, 3
    vmem, anywhere = pl.BlockSpec(memory_space=pltpu.VMEM), pl.BlockSpec(memory_space=pl.ANY)
    sems = pltpu.SemaphoreType.DMA
    return pl.pallas_call(
        functools.partial(relay_kernel, sections, cut),
        out_shape=jax.ShapeDtypeStruct((1, ticks, rows, width), jnp.bfloat16),
        in_specs=[anywhere, anywhere, vmem, vmem, vmem, anywhere, anywhere],
        out_specs=vmem,
        scratch_shapes=[
            pltpu.VMEM((ticks, 2, rows, width), jnp.bfloat16),
            pltpu.VMEM((ticks, 2, rows, width), jnp.bfloat16),
            pltpu.VMEM((ticks, 2, rows, width), jnp.bfloat16),
            pltpu.VMEM((ticks - 1, 2, rows, width), jnp.bfloat16),
            pltpu.VMEM((ticks, 1, rows), jnp.int32),
            pltpu.VMEM((width, hid), jnp.bfloat16),
            pltpu.VMEM((hid, width), jnp.bfloat16),
            pltpu.VMEM((width, hid), jnp.bfloat16),
            pltpu.VMEM((hid, width), jnp.bfloat16),
            pltpu.VMEM((2 * rows, width), jnp.float32),
            pltpu.VMEM((2 * rows, 2 * hid), jnp.bfloat16),
            pltpu.VMEM((2 * rows, 1), jnp.float32),
            sems((2 + ticks,)),
            sems((2, 1 + ticks)),
            sems((2, up_cut)),
            sems((2, up_cut)),
            sems((2, cut)),
            sems((2, cut)),
            sems((2, ticks, cut)),
            sems((2, ticks - 1, cut)),
        ],
        compiler_params=pltpu.CompilerParams(
            collective_id=0, has_side_effects=True, vmem_limit_bytes=63 * 2**20
        ),
    )(
        pending_microgroups,
        arriving_microgroups,
        expert_choice_grid,
        rootmean_gain,
        jnp.swapaxes(gating_columns, 1, 2),
        up_projection_matrix,
        down_projection_matrix,
    )


def solution(mesh):
    placed = (
        P("section", ("groups", "expert"), None),
        P(None, ("groups", "expert"), None),
        P(None, "section", ("groups", "expert")),
        P("section", None),
        P("section", None, None),
        P("section", "expert", None, None),
        P("section", "expert", None, None),
    )
    shape = dict(mesh.shape)
    if shape["expert"] == 4 and shape["groups"] == 2:
        form = functools.partial(relay, shape["section"])
    else:
        form = per_device
    return jax.shard_map(
        form,
        mesh=mesh,
        in_specs=placed,
        out_specs=P("section", None, ("groups", "expert"), None),
        check_vma=False,
    )
```
